32 devices in a mesh: tm: 8 (over z, core), bat: 4 (over y, x).
Axes of the slice: x: 2, y: 2, z: 4, core: 2. Of those that a mesh axis runs over, the one named last changes fastest.
Arguments:
- power0: float32 [128, 1536], P('tm', 'bat'), may hold values from -0.5 to 0.5
- charge0: float32 [128, 1536], P('tm', 'bat'), may hold values from 0 to 1
- dyn_dual0: float32 [128, 1536], P('tm', 'bat'), may hold values from -3 to 3
- feeder_dual0: float32 [128, 768], P(('tm', 'bat')), may hold values from 0 to 0.5
- price: float32 [128, 1536], P('tm', 'bat'), may hold values from -12 to 12
- inflow: float32 [128, 1536], P('tm', 'bat'), may hold values from -1.5 to 1.5
- power_limit: float32 [1536], P('bat'), may hold values from 0.5 to 6
- capacity: float32 [1536], P('bat'), may hold values from 0.5 to 8
- feeder_limit: float32 [768], replicated, may hold values from 0 to 1
- block_values: float32 [18, 128, 128], replicated, may hold values from -0.3125 to 0.3125
- block_cols: int32 [18], replicated, may hold values from 0 to 11, as said below
- block_offsets: int32 [7], replicated, may hold values from 0 to 18, as said below
Outputs:
- power: float32 [128, 1536], P('tm', 'bat')
- charge: float32 [128, 1536], P('tm', 'bat')
- dyn_dual: float32 [128, 1536], P('tm', 'bat')
- feeder_dual: float32 [128, 768], P(('tm', 'bat'))
The draws below stay inside these ranges and needn't reach their ends.
Inputs may be any that keep to these rules, and one draw needn't show every extreme that they name: `block_cols`: every battery block 0 to 11 appears at least once. block_offsets[0] = 0, strictly rising, block_offsets[6] = 18.
All inputs are finite; a program needn't handle non-finite values.
Results may differ from the reference program's by a relative error of at most 0.0001.
Values sent between devices are 32-bit elements; how exact they have to be, the bound alone decides.
A program may use at most 64 MiB of HBM per device.

```python
import math
import jax
import jax.numpy as jnp
from jax import lax

BLK = 128
ITERS = 4
T_SIZE = 128
B = 1536
NB = 12
FEED_BLK = 6
NNZB = 18
FR = 768


def draw_price(key, part):
    ramp = 1.0 + 2.0 * jnp.arange(T_SIZE, dtype=jnp.float32) / max(T_SIZE - 1, 1)
    base = jnp.clip(jax.random.normal(key, (T_SIZE, B), jnp.float32), -3.5, 3.5)
    return base * ramp[:, None]


def draw_power_limit(key, part):
    ramp = 1.0 + 2.0 * jnp.arange(B, dtype=jnp.float32) / max(B - 1, 1)
    base = jnp.exp(jax.random.uniform(key, (B,), jnp.float32, jnp.log(0.5), jnp.log(2.0)))
    return base * ramp


def draw_block_cols(key, part):
    first = jax.random.permutation(jax.random.fold_in(key, 11), NB)
    extra = jax.random.randint(jax.random.fold_in(key, 12), (NNZB - NB,), 0, NB)
    joined = jnp.concatenate([first, extra]).astype(jnp.int32)
    return jax.random.permutation(jax.random.fold_in(key, 13), joined).astype(jnp.int32)


def draw_block_offsets(key, part):
    picks = jax.random.permutation(jax.random.fold_in(key, 21), NNZB - 1)[:FEED_BLK - 1] + 1
    cuts = jnp.sort(picks.astype(jnp.int32))
    head = jnp.zeros((1,), jnp.int32)
    tail = jnp.full((1,), NNZB, jnp.int32)
    return jnp.concatenate([head, cuts, tail]).astype(jnp.int32)


def block_levels(rng, dims, shards, low, high):
    factor_of, own = 1.0, jax.random.fold_in(rng, 6)
    for dim, parts in shards:
        heights = jnp.exp(jax.random.uniform(jax.random.fold_in(own, dim), (parts,), jnp.float32, low / len(shards), high / len(shards)))
        factor_of = factor_of * jnp.repeat(heights, dims[dim] // parts).reshape([-1 if axis == dim else 1 for axis in range(len(dims))])
    return factor_of


def noise(own_key, extent, deviation, reach, pieces=(), kind=jnp.bfloat16):
    loudness = block_levels(own_key, extent, pieces, -0.22, 0.18) if pieces else 1.0
    result = jax.random.normal(own_key, extent, jnp.float32) * deviation * loudness
    return jnp.minimum(jnp.maximum(result, -reach), reach).astype(kind)


def setup_inputs(seed: int = 0) -> dict:
    key_list = jax.random.split(jax.random.key(seed), 13)
    return {
        "power0": jnp.clip(jax.random.uniform(key_list[0], (T_SIZE, B), jnp.float32, -0.5, 0.5) * block_levels(key_list[0], (T_SIZE, B), ((0, 8), (1, 4)), -0.4, 0.0), -0.5, 0.5),
        "charge0": jnp.clip(1.0 * jax.random.uniform(key_list[1], (T_SIZE, B), jnp.float32) ** block_levels(key_list[1], (T_SIZE, B), ((0, 8), (1, 4)), -0.2, 0.2), 0.0, 1.0),
        "dyn_dual0": noise(key_list[2], (T_SIZE, B), 0.5, 3.0, ((0, 8), (1, 4)), jnp.float32),
        "feeder_dual0": jnp.clip(0.5 * jax.random.uniform(key_list[3], (T_SIZE, FR), jnp.float32) ** block_levels(key_list[3], (T_SIZE, FR), ((0, 32),), -0.2, 0.2), 0.0, 0.5),
        "price": draw_price(jax.random.fold_in(key_list[12], 71), 0),
        "inflow": noise(key_list[5], (T_SIZE, B), 0.3, 1.5, ((0, 8), (1, 4)), jnp.float32),
        "power_limit": draw_power_limit(jax.random.fold_in(key_list[12], 71), 0),
        "capacity": jnp.clip(jnp.exp(math.log(8.0) - 2.7725887 * jax.random.uniform(key_list[7], (B,), jnp.float32) ** block_levels(key_list[7], (B,), ((0, 4),), -0.2, 0.2)), 0.5, 8.0),
        "feeder_limit": jnp.clip(jax.random.uniform(key_list[8], (FR,), jnp.float32, 0.0, 1.0), 0.0, 1.0),
        "block_values": noise(key_list[9], (NNZB, BLK, BLK), (3 * BLK) ** -0.5, 0.3125, (), jnp.float32),
        "block_cols": draw_block_cols(jax.random.fold_in(key_list[12], 71), 0),
        "block_offsets": draw_block_offsets(jax.random.fold_in(key_list[12], 71), 0),
    }


HIGH = lax.Precision.HIGHEST
ETA_STEP = 0.4
EPS_NORM = 1e-06

def row_table(block_offsets, count, dtype):
    index_all = jnp.arange(count, dtype=jnp.int32)
    row_of = lax.optimization_barrier(jnp.sum((index_all[:, None] >= block_offsets[None, 1:-1]).astype(jnp.int32), axis=1))
    feed_count = block_offsets.shape[0] - 1
    return (row_of[:, None] == jnp.arange(feed_count, dtype=jnp.int32)[None, :]).astype(dtype)

def column_table(block_cols, battery_blocks, dtype):
    return (block_cols[:, None] == jnp.arange(battery_blocks, dtype=jnp.int32)[None, :]).astype(dtype)

def feeder_apply(field, block_values, rows_tab, cols_tab):
    count_rows = field.shape[0]
    blk = block_values.shape[1]
    blocks = field.reshape(count_rows, -1, blk)
    picked = jnp.einsum('rnk,jn->rjk', blocks, cols_tab, precision=HIGH)
    partial_rows = jnp.einsum('rjk,jmk->rjm', picked, block_values, precision=HIGH)
    summed = jnp.einsum('rjm,jf->rfm', partial_rows, rows_tab, precision=HIGH)
    return summed.reshape(count_rows, -1)

def feeder_adjoint(duals, block_values, rows_tab, cols_tab):
    count_rows = duals.shape[0]
    blk = block_values.shape[1]
    blocks = duals.reshape(count_rows, -1, blk)
    chosen = jnp.einsum('rfm,jf->rjm', blocks, rows_tab, precision=HIGH)
    pushed = jnp.einsum('rjm,jmk->rjk', chosen, block_values, precision=HIGH)
    spread = jnp.einsum('rjk,jn->rnk', pushed, cols_tab, precision=HIGH)
    return spread.reshape(count_rows, -1)

def reference(power0, charge0, dyn_dual0, feeder_dual0, price, inflow, power_limit, capacity, feeder_limit, block_values, block_cols, block_offsets):
    dtype = power0.dtype
    blk = block_values.shape[1]
    rows_tab = row_table(block_offsets, block_values.shape[0], dtype)
    cols_tab = column_table(block_cols, power0.shape[1] // blk, dtype)
    power, charge, dyn_dual, feeder_dual = (power0, charge0, dyn_dual0, feeder_dual0)
    weight = jnp.asarray(1.0, dtype=dtype)
    pushed = feeder_adjoint(feeder_dual, block_values, rows_tab, cols_tab)
    zero_row = jnp.zeros((1, power0.shape[1]), dtype)
    for iteration in range(ITERS):
        step_primal = ETA_STEP / weight
        step_dual = ETA_STEP * weight
        dual_next = jnp.concatenate([dyn_dual[1:], zero_row], axis=0)
        power_new = jnp.clip(power - step_primal * (price - dyn_dual + pushed), -power_limit[None, :], power_limit[None, :])
        charge_new = jnp.clip(charge - step_primal * (dyn_dual - dual_next), 0.0, capacity[None, :])
        power_bar = 2.0 * power_new - power
        charge_bar = 2.0 * charge_new - charge
        charge_prev = jnp.concatenate([zero_row, charge_bar[:-1]], axis=0)
        dyn_new = dyn_dual + step_dual * (charge_bar - charge_prev - power_bar - inflow)
        feeder_new = jnp.maximum(0.0, feeder_dual + step_dual * (feeder_apply(power_bar, block_values, rows_tab, cols_tab) - feeder_limit[None, :]))
        if iteration + 1 < ITERS:
            move_power = power_new - power
            move_charge = charge_new - charge
            primal_sq = jnp.sum(move_power * move_power + move_charge * move_charge)
            move_dyn = dyn_new - dyn_dual
            move_feed = feeder_new - feeder_dual
            dual_sq = jnp.sum(move_dyn * move_dyn) + jnp.sum(move_feed * move_feed)
            weight = jnp.sqrt(weight * jnp.sqrt((dual_sq + EPS_NORM) / (primal_sq + EPS_NORM)))
            pushed = feeder_adjoint(feeder_new, block_values, rows_tab, cols_tab)
        power, charge, dyn_dual, feeder_dual = (power_new, charge_new, dyn_new, feeder_new)
    return (power, charge, dyn_dual, feeder_dual)
```

```python
import functools

import jax
import jax.numpy as jnp
from jax import lax
from jax.experimental import pallas as pl
from jax.experimental.pallas import tpu as pltpu
from jax.sharding import PartitionSpec as P

ITERS = 4
ETA_STEP = 0.4
EPS_NORM = 1e-06
MESH = pl.DeviceIdType.MESH
F32, BF16 = jnp.float32, jnp.bfloat16


def split(x):
    high = x.astype(BF16)
    return high, (x - high.astype(F32)).astype(BF16)


def stacked(x, axis):
    return jnp.concatenate(split(x), axis=axis)


def quadrants(out, rows, blk):
    return out[:rows, :blk] + (out[rows:, :blk] + out[:rows, blk:])


def kernel(
    tm_n, bat_n,
    power_ref, charge_ref, dyn_ref, feed_ref, price_ref, inflow_ref,
    limit_ref, capacity_ref, feed_limit_ref, values_ref, cols_ref, offsets_ref,
    power_out, charge_out, dyn_out, feed_out,
    feed_all, bars, bar_parts, feed_parts, running, by_rows, by_cols,
    sums, row_next, row_prev, row_charge, own_first, own_last, own_charge, feed_own,
    feed_send, feed_recv, bar_send, bar_recv, sum_send, sum_recv, edge_send, edge_recv,
):
    me_t, me_b = lax.axis_index("tm"), lax.axis_index("bat")
    rows, cols = power_ref.shape
    stored, blk, _ = values_ref.shape
    own = cols // blk
    feed_blocks = feed_ref.shape[1] // blk
    feed_rows = feed_ref.shape[0]
    tiles = rows // 8
    group = own * tiles + 1

    def bat_at(d):
        return (me_t, lax.rem(me_b + d, bat_n))

    def tm_at(d):
        return (lax.rem(me_t + d, tm_n), me_b)

    barrier = pltpu.get_barrier_semaphore()
    for d in range(1, bat_n):
        pl.semaphore_signal(barrier, inc=1, device_id=bat_at(d), device_id_type=MESH)
    for d in range(1, tm_n):
        pl.semaphore_signal(barrier, inc=1, device_id=tm_at(d), device_id_type=MESH)
    pl.semaphore_wait(barrier, bat_n + tm_n - 2)

    started = []

    def send(src, dst, send_sem, recv_sem, device):
        copy = pltpu.make_async_remote_copy(
            src_ref=src, dst_ref=dst, send_sem=send_sem, recv_sem=recv_sem,
            device_id=device, device_id_type=MESH,
        )
        copy.start()
        started.append(copy)
        return copy

    def part(ref, k):
        return ref[:, k * blk:(k + 1) * blk]

    feed_copies = [
        send(feed_ref, feed_all.at[me_b], feed_send.at[d - 1], feed_recv.at[d - 1], bat_at(d))
        for d in range(1, bat_n)
    ]
    own_first[0] = dyn_ref[0:1, :]
    own_last[0] = dyn_ref[rows - 1:rows, :]
    own_charge[...] = charge_ref[rows - 1:rows, :]

    def send_edges(step):
        return [
            send(own_first.at[step], row_next.at[step],
                 edge_send.at[2 * step], edge_recv.at[2 * step], tm_at(tm_n - 1)),
            send(own_last.at[step], row_prev.at[step],
                 edge_send.at[2 * step + 1], edge_recv.at[2 * step + 1], tm_at(1)),
        ]

    edge_copies = send_edges(0) + [
        send(own_charge, row_charge, edge_send.at[2 * ITERS], edge_recv.at[2 * ITERS], tm_at(1))
    ]

    feed_all[me_b] = feed_ref[...]
    for j in range(stored):
        high, low = split(values_ref[j])
        by_cols[j, :, :blk] = high
        by_cols[j, :, blk:] = low
        by_rows[j, :blk, :] = high
        by_rows[j, blk:, :] = low

    row_of = [
        sum((j >= offsets_ref[f]).astype(jnp.int32) for f in range(1, feed_blocks))
        for j in range(stored)
    ]
    col_of = [cols_ref[j] for j in range(stored)]
    inside = [
        [(col_of[j] == me_b * own + k).astype(F32) for k in range(own)] for j in range(stored)
    ]

    def battery_of(feed):
        for f in range(feed_blocks):
            feed_parts[f] = stacked(feed[f], 0)
        total = [jnp.zeros((rows, blk), F32) for _ in range(own)]
        for j in range(stored):
            out = jnp.dot(feed_parts[row_of[j]], by_cols[j], preferred_element_type=F32)
            out = quadrants(out, rows, blk)
            for k in range(own):
                total[k] = total[k] + inside[j][k] * out
        return total

    def feeder_of():
        total = jnp.zeros((rows, blk), F32)
        running[0] = total
        for j in range(stored):
            out = lax.dot_general(
                bar_parts[col_of[j]], by_rows[j], (((1,), (1,)), ((), ())),
                preferred_element_type=F32,
            )
            total = total + quadrants(out, rows, blk)
            running[j + 1] = total
        return [running[offsets_ref[f + 1]] - running[offsets_ref[f]] for f in range(feed_blocks)]

    for copy in feed_copies:
        copy.wait_recv()
    feed = [
        jnp.concatenate([feed_all[n, :, f * blk:(f + 1) * blk] for n in range(bat_n)], axis=0)
        for f in range(feed_blocks)
    ]
    pushed = battery_of(feed)

    for copy in edge_copies:
        copy.wait_recv()

    index = lax.broadcasted_iota(jnp.int32, (rows, blk), 0)
    not_first = jnp.where(me_t == 0, 0.0, 1.0)
    not_last = jnp.where(me_t == tm_n - 1, 0.0, 1.0)
    power = [part(power_ref, k) for k in range(own)]
    charge = [part(charge_ref, k) for k in range(own)]
    dyn = [part(dyn_ref, k) for k in range(own)]
    before = [part(row_charge, k) for k in range(own)]
    weight = jnp.ones((1, blk), F32)

    for step in range(ITERS):
        last = step + 1 == ITERS
        step_primal = ETA_STEP / weight
        step_dual = ETA_STEP * weight
        primal = jnp.zeros((rows, blk), F32)
        moved = jnp.zeros((rows, blk), F32)
        power_new, charge_new, dyn_new, before_new = [], [], [], []
        for k in range(own):
            limit, capacity = part(limit_ref, k), part(capacity_ref, k)
            here = dyn[k]
            following = row_next[step, :, k * blk:(k + 1) * blk] * not_last
            preceding = row_prev[step, :, k * blk:(k + 1) * blk]
            later = jnp.where(index == rows - 1, following, pltpu.roll(here, rows - 1, 0))
            p = power[k] - step_primal * (part(price_ref, k) - here + pushed[k])
            p = jnp.minimum(jnp.maximum(p, -limit), limit)
            c = charge[k] - step_primal * (here - later)
            c = jnp.minimum(jnp.maximum(c, 0.0), capacity)
            b = before[k] - step_primal * (preceding - here[0:1])
            b = jnp.minimum(jnp.maximum(b, 0.0), capacity)
            power_bar = 2.0 * p - power[k]
            charge_bar = 2.0 * c - charge[k]
            before_bar = (2.0 * b - before[k]) * not_first
            earlier = jnp.where(index == 0, before_bar, pltpu.roll(charge_bar, 1, 0))
            n = here + step_dual * (charge_bar - earlier - power_bar - part(inflow_ref, k))
            bars[step, pl.ds(me_b * group + k * tiles, tiles)] = power_bar.reshape(tiles, 8, blk)
            if not last:
                primal = primal + ((p - power[k]) * (p - power[k]) + (c - charge[k]) * (c - charge[k]))
                moved = moved + (n - here) * (n - here)
            power_new.append(p)
            charge_new.append(c)
            dyn_new.append(n)
            before_new.append(b)
        spare = jnp.zeros((6, blk), F32)
        bars[step, me_b * group + own * tiles] = jnp.concatenate(
            [jnp.sum(primal, axis=0, keepdims=True), jnp.sum(moved, axis=0, keepdims=True), spare], axis=0
        )
        mine = bars.at[step, pl.ds(me_b * group, group)]
        bar_copies = [
            send(mine, mine, bar_send.at[step, d - 1], bar_recv.at[step, d - 1], bat_at(d))
            for d in range(1, bat_n)
        ]
        if not last:
            for k in range(own):
                own_first[step + 1, :, k * blk:(k + 1) * blk] = dyn_new[k][0:1]
                own_last[step + 1, :, k * blk:(k + 1) * blk] = dyn_new[k][rows - 1:rows]
            edge_copies = send_edges(step + 1)
        else:
            for k in range(own):
                power_out[:, k * blk:(k + 1) * blk] = power_new[k]
                charge_out[:, k * blk:(k + 1) * blk] = charge_new[k]
                dyn_out[:, k * blk:(k + 1) * blk] = dyn_new[k]
        for copy in bar_copies:
            copy.wait_recv()
        for n in range(bat_n):
            for k in range(own):
                start = n * group + k * tiles
                bar_parts[n * own + k] = stacked(
                    bars[step, start:start + tiles].reshape(rows, blk), 0
                )
        coupled = feeder_of()
        feed_new = [
            jnp.maximum(0.0, feed[f] + step_dual * (coupled[f] - part(feed_limit_ref, f)))
            for f in range(feed_blocks)
        ]
        if not last:
            change = jnp.zeros((rows, blk), F32)
            for f in range(feed_blocks):
                change = change + (feed_new[f] - feed[f]) * (feed_new[f] - feed[f])
            change = jnp.sum(change, axis=0, keepdims=True)
            gathered = bars[step, group - 1]
            for n in range(1, bat_n):
                gathered = gathered + bars[step, n * group + group - 1]
            sums[step, me_t] = jnp.concatenate([gathered[0:1], gathered[1:2] + change], axis=0)
            total = sums.at[step, me_t]
            sum_copies = [
                send(total, total, sum_send.at[step, d - 1], sum_recv.at[step, d - 1], tm_at(d))
                for d in range(1, tm_n)
            ]
            pushed = battery_of(feed_new)
            for copy in sum_copies + edge_copies:
                copy.wait_recv()
            both = sums[step, 0]
            for t in range(1, tm_n):
                both = both + sums[step, t]
            both = jnp.sum(both, axis=1, keepdims=True) + EPS_NORM
            ratio = jnp.sqrt(jnp.broadcast_to(both[1:2], (1, blk)) / jnp.broadcast_to(both[0:1], (1, blk)))
            weight = jnp.sqrt(weight * ratio)
        power, charge, dyn, before, feed = power_new, charge_new, dyn_new, before_new, feed_new

    for n in range(bat_n):
        for f in range(feed_blocks):
            feed_own[n, :, f * blk:(f + 1) * blk] = feed[f][n * feed_rows:(n + 1) * feed_rows]
    feed_out[...] = feed_own[me_b]
    for copy in started:
        copy.wait_send()


def shards(
    tm_n, bat_n, power0, charge0, dyn_dual0, feeder_dual0, price, inflow,
    power_limit, capacity, feeder_limit, block_values, block_cols, block_offsets,
):
    rows, cols = power0.shape
    stored, blk, _ = block_values.shape
    feed_rows, feed_cols = feeder_dual0.shape
    own, feed_blocks = cols // blk, feed_cols // blk
    group = own * (rows // 8) + 1
    vmem = pl.BlockSpec(memory_space=pltpu.VMEM)
    smem = pl.BlockSpec(memory_space=pltpu.SMEM)
    dma = pltpu.SemaphoreType.DMA
    state = jax.ShapeDtypeStruct((rows, cols), F32)
    return pl.pallas_call(
        functools.partial(kernel, tm_n, bat_n),
        out_shape=(state, state, state, jax.ShapeDtypeStruct((feed_rows, feed_cols), F32)),
        in_specs=[vmem] * 10 + [smem] * 2,
        out_specs=(vmem,) * 4,
        scratch_shapes=[
            pltpu.VMEM((bat_n, feed_rows, feed_cols), F32),
            pltpu.VMEM((ITERS, bat_n * group, 8, blk), F32),
            pltpu.VMEM((bat_n * own, 2 * rows, blk), BF16),
            pltpu.VMEM((feed_blocks, 2 * rows, blk), BF16),
            pltpu.VMEM((stored + 1, rows, blk), F32),
            pltpu.VMEM((stored, 2 * blk, blk), BF16),
            pltpu.VMEM((stored, blk, 2 * blk), BF16),
            pltpu.VMEM((ITERS - 1, tm_n, 2, blk), F32),
            pltpu.VMEM((ITERS, 1, cols), F32),
            pltpu.VMEM((ITERS, 1, cols), F32),
            pltpu.VMEM((1, cols), F32),
            pltpu.VMEM((ITERS, 1, cols), F32),
            pltpu.VMEM((ITERS, 1, cols), F32),
            pltpu.VMEM((1, cols), F32),
            pltpu.VMEM((bat_n, feed_rows, feed_cols), F32),
            dma((bat_n - 1,)), dma((bat_n - 1,)),
            dma((ITERS, bat_n - 1)), dma((ITERS, bat_n - 1)),
            dma((ITERS - 1, tm_n - 1)), dma((ITERS - 1, tm_n - 1)),
            dma((2 * ITERS + 1,)), dma((2 * ITERS + 1,)),
        ],
        compiler_params=pltpu.CompilerParams(
            collective_id=0, has_side_effects=True, vmem_limit_bytes=48 * 1024 * 1024
        ),
    )(
        power0, charge0, dyn_dual0, feeder_dual0, price, inflow,
        power_limit.reshape(1, -1), capacity.reshape(1, -1), feeder_limit.reshape(1, -1),
        block_values, block_cols, block_offsets,
    )


def solution(mesh):
    state = P("tm", "bat")
    duals = P(("tm", "bat"), None)
    return jax.shard_map(
        functools.partial(shards, mesh.shape["tm"], mesh.shape["bat"]),
        mesh=mesh,
        in_specs=(state, state, state, duals, state, state, P("bat"), P("bat"), P(), P(), P(), P()),
        out_specs=(state, state, state, duals),
        check_vma=False,
    )
```

```python
import functools

import jax
import jax.numpy as jnp
from jax import lax
from jax.experimental import pallas as pl
from jax.experimental.pallas import tpu as pltpu
from jax.sharding import PartitionSpec as P

ITERS = 4
ETA_STEP = 0.4
EPS_NORM = 1e-06
VMEM_BYTES = 64 * 1024 * 1024
MESH = pl.DeviceIdType.MESH
F32, BF16 = jnp.float32, jnp.bfloat16


def split(x):
    high = x.astype(BF16)
    return high, (x - high.astype(F32)).astype(BF16)


def stacked(x, axis):
    return jnp.concatenate(split(x), axis=axis)


def quadrants(out, rows, blk):
    return out[:rows, :blk] + (out[rows:, :blk] + out[:rows, blk:])


def kernel(
    tm_n, bat_n,
    power_in, charge_in, dyn_in, feed_in, price_in, inflow_in,
    limit_in, capacity_in, feed_limit_in, values_in, cols_in, offsets_in,
    power_out, charge_out, dyn_out, feed_out,
    power_ref, charge_ref, dyn_ref, feed_ref, price_ref, inflow_ref,
    limit_ref, capacity_ref, feed_limit_ref, values_ref, cols_ref, offsets_ref, fetch_sem,
    feed_all, bars, bar_parts, feed_parts, running, by_rows, by_cols,
    sums, row_next, row_prev, row_charge, own_first, own_last, own_charge, feed_own,
    feed_send, feed_recv, bar_send, bar_recv, sum_send, sum_recv, edge_send, edge_recv,
):
    me_t, me_b = lax.axis_index("tm"), lax.axis_index("bat")
    pairs = (
        (feed_in, feed_ref), (dyn_in, dyn_ref), (charge_in, charge_ref), (values_in, values_ref),
        (cols_in, cols_ref), (offsets_in, offsets_ref), (power_in, power_ref), (price_in, price_ref),
        (inflow_in, inflow_ref), (limit_in, limit_ref), (capacity_in, capacity_ref),
        (feed_limit_in, feed_limit_ref),
    )
    fetches = [pltpu.make_async_copy(a, b, fetch_sem.at[i]) for i, (a, b) in enumerate(pairs)]
    for copy in fetches:
        copy.start()
    rows, cols = power_ref.shape
    stored, blk, _ = values_ref.shape
    own = cols // blk
    feed_blocks = feed_ref.shape[1] // blk
    feed_rows = feed_ref.shape[0]
    tiles = rows // 8
    group = own * tiles + 1

    def bat_at(d):
        return (me_t, lax.rem(me_b + d, bat_n))

    def tm_at(d):
        return (lax.rem(me_t + d, tm_n), me_b)

    barrier = pltpu.get_barrier_semaphore()
    for d in range(1, bat_n):
        pl.semaphore_signal(barrier, inc=1, device_id=bat_at(d), device_id_type=MESH)
    for d in range(1, tm_n):
        pl.semaphore_signal(barrier, inc=1, device_id=tm_at(d), device_id_type=MESH)
    pl.semaphore_wait(barrier, bat_n + tm_n - 2)

    started = []

    def send(src, dst, send_sem, recv_sem, device):
        copy = pltpu.make_async_remote_copy(
            src_ref=src, dst_ref=dst, send_sem=send_sem, recv_sem=recv_sem,
            device_id=device, device_id_type=MESH,
        )
        copy.start()
        started.append(copy)
        return copy

    def part(ref, k):
        return ref[:, k * blk:(k + 1) * blk]

    def row_part(ref, k):
        return ref[k * blk:(k + 1) * blk].reshape(1, blk)

    fetches[0].wait()
    feed_copies = [
        send(feed_ref, feed_all.at[me_b], feed_send.at[d - 1], feed_recv.at[d - 1], bat_at(d))
        for d in range(1, bat_n)
    ]
    fetches[1].wait()
    fetches[2].wait()
    own_first[0] = dyn_ref[0:1, :]
    own_last[0] = dyn_ref[rows - 1:rows, :]
    own_charge[...] = charge_ref[rows - 1:rows, :]

    def send_edges(step):
        return [
            send(own_first.at[step], row_next.at[step],
                 edge_send.at[2 * step], edge_recv.at[2 * step], tm_at(tm_n - 1)),
            send(own_last.at[step], row_prev.at[step],
                 edge_send.at[2 * step + 1], edge_recv.at[2 * step + 1], tm_at(1)),
        ]

    edge_copies = send_edges(0) + [
        send(own_charge, row_charge, edge_send.at[2 * ITERS], edge_recv.at[2 * ITERS], tm_at(1))
    ]

    feed_all[me_b] = feed_ref[...]
    for copy in fetches[3:]:
        copy.wait()
    for j in range(stored):
        high, low = split(values_ref[j])
        by_cols[j, :, :blk] = high
        by_cols[j, :, blk:] = low
        by_rows[j, :blk, :] = high
        by_rows[j, blk:, :] = low

    row_of = [
        sum((j >= offsets_ref[f]).astype(jnp.int32) for f in range(1, feed_blocks))
        for j in range(stored)
    ]
    col_of = [cols_ref[j] for j in range(stored)]
    inside = [
        [(col_of[j] == me_b * own + k).astype(F32) for k in range(own)] for j in range(stored)
    ]

    def battery_of(feed):
        for f in range(feed_blocks):
            feed_parts[f] = stacked(feed[f], 0)
        total = [jnp.zeros((rows, blk), F32) for _ in range(own)]
        for j in range(stored):
            out = jnp.dot(feed_parts[row_of[j]], by_cols[j], preferred_element_type=F32)
            out = quadrants(out, rows, blk)
            for k in range(own):
                total[k] = total[k] + inside[j][k] * out
        return total

    def feeder_of():
        total = jnp.zeros((rows, blk), F32)
        running[0] = total
        for j in range(stored):
            out = lax.dot_general(
                bar_parts[col_of[j]], by_rows[j], (((1,), (1,)), ((), ())),
                preferred_element_type=F32,
            )
            total = total + quadrants(out, rows, blk)
            running[j + 1] = total
        return [running[offsets_ref[f + 1]] - running[offsets_ref[f]] for f in range(feed_blocks)]

    for copy in feed_copies:
        copy.wait_recv()
    feed = [
        jnp.concatenate([feed_all[n, :, f * blk:(f + 1) * blk] for n in range(bat_n)], axis=0)
        for f in range(feed_blocks)
    ]
    pushed = battery_of(feed)

    for copy in edge_copies:
        copy.wait_recv()

    index = lax.broadcasted_iota(jnp.int32, (rows, blk), 0)
    not_first = jnp.where(me_t == 0, 0.0, 1.0)
    not_last = jnp.where(me_t == tm_n - 1, 0.0, 1.0)
    power = [part(power_ref, k) for k in range(own)]
    charge = [part(charge_ref, k) for k in range(own)]
    dyn = [part(dyn_ref, k) for k in range(own)]
    before = [part(row_charge, k) for k in range(own)]
    weight = jnp.ones((1, blk), F32)

    for step in range(ITERS):
        last = step + 1 == ITERS
        step_primal = ETA_STEP / weight
        step_dual = ETA_STEP * weight
        primal = jnp.zeros((rows, blk), F32)
        moved = jnp.zeros((rows, blk), F32)
        power_new, charge_new, dyn_new, before_new = [], [], [], []
        for k in range(own):
            limit, capacity = row_part(limit_ref, k), row_part(capacity_ref, k)
            here = dyn[k]
            following = row_next[step, :, k * blk:(k + 1) * blk] * not_last
            preceding = row_prev[step, :, k * blk:(k + 1) * blk]
            later = jnp.where(index == rows - 1, following, pltpu.roll(here, rows - 1, 0))
            p = power[k] - step_primal * (part(price_ref, k) - here + pushed[k])
            p = jnp.minimum(jnp.maximum(p, -limit), limit)
            c = charge[k] - step_primal * (here - later)
            c = jnp.minimum(jnp.maximum(c, 0.0), capacity)
            b = before[k] - step_primal * (preceding - here[0:1])
            b = jnp.minimum(jnp.maximum(b, 0.0), capacity)
            power_bar = 2.0 * p - power[k]
            charge_bar = 2.0 * c - charge[k]
            before_bar = (2.0 * b - before[k]) * not_first
            earlier = jnp.where(index == 0, before_bar, pltpu.roll(charge_bar, 1, 0))
            n = here + step_dual * (charge_bar - earlier - power_bar - part(inflow_ref, k))
            bars[step, pl.ds(me_b * group + k * tiles, tiles)] = power_bar.reshape(tiles, 8, blk)
            if not last:
                primal = primal + ((p - power[k]) * (p - power[k]) + (c - charge[k]) * (c - charge[k]))
                moved = moved + (n - here) * (n - here)
            power_new.append(p)
            charge_new.append(c)
            dyn_new.append(n)
            before_new.append(b)
        spare = jnp.zeros((6, blk), F32)
        bars[step, me_b * group + own * tiles] = jnp.concatenate(
            [jnp.sum(primal, axis=0, keepdims=True), jnp.sum(moved, axis=0, keepdims=True), spare], axis=0
        )
        mine = bars.at[step, pl.ds(me_b * group, group)]
        bar_copies = [
            send(mine, mine, bar_send.at[step, d - 1], bar_recv.at[step, d - 1], bat_at(d))
            for d in range(1, bat_n)
        ]
        if not last:
            for k in range(own):
                own_first[step + 1, :, k * blk:(k + 1) * blk] = dyn_new[k][0:1]
                own_last[step + 1, :, k * blk:(k + 1) * blk] = dyn_new[k][rows - 1:rows]
            edge_copies = send_edges(step + 1)
        else:
            for k in range(own):
                power_out[:, k * blk:(k + 1) * blk] = power_new[k]
                charge_out[:, k * blk:(k + 1) * blk] = charge_new[k]
                dyn_out[:, k * blk:(k + 1) * blk] = dyn_new[k]
        for copy in bar_copies:
            copy.wait_recv()
        for n in range(bat_n):
            for k in range(own):
                start = n * group + k * tiles
                bar_parts[n * own + k] = stacked(
                    bars[step, start:start + tiles].reshape(rows, blk), 0
                )
        coupled = feeder_of()
        feed_new = [
            jnp.maximum(0.0, feed[f] + step_dual * (coupled[f] - row_part(feed_limit_ref, f)))
            for f in range(feed_blocks)
        ]
        if not last:
            change = jnp.zeros((rows, blk), F32)
            for f in range(feed_blocks):
                change = change + (feed_new[f] - feed[f]) * (feed_new[f] - feed[f])
            change = jnp.sum(change, axis=0, keepdims=True)
            gathered = bars[step, group - 1]
            for n in range(1, bat_n):
                gathered = gathered + bars[step, n * group + group - 1]
            sums[step, me_t] = jnp.concatenate([gathered[0:1], gathered[1:2] + change], axis=0)
            total = sums.at[step, me_t]
            sum_copies = [
                send(total, total, sum_send.at[step, d - 1], sum_recv.at[step, d - 1], tm_at(d))
                for d in range(1, tm_n)
            ]
            pushed = battery_of(feed_new)
            for copy in sum_copies + edge_copies:
                copy.wait_recv()
            both = sums[step, 0]
            for t in range(1, tm_n):
                both = both + sums[step, t]
            both = jnp.sum(both, axis=1, keepdims=True) + EPS_NORM
            ratio = jnp.sqrt(jnp.broadcast_to(both[1:2], (1, blk)) / jnp.broadcast_to(both[0:1], (1, blk)))
            weight = jnp.sqrt(weight * ratio)
        power, charge, dyn, before, feed = power_new, charge_new, dyn_new, before_new, feed_new

    for n in range(bat_n):
        for f in range(feed_blocks):
            feed_own[n, :, f * blk:(f + 1) * blk] = feed[f][n * feed_rows:(n + 1) * feed_rows]
    feed_out[...] = feed_own[me_b]
    for copy in started:
        copy.wait_send()


def hand_over(*refs):
    half = (len(refs) - 1) // 2
    sem = refs[-1]
    copies = [
        pltpu.make_async_copy(a, b, sem.at[i])
        for i, (a, b) in enumerate(zip(refs[:half], refs[half:-1]))
    ]
    for copy in copies:
        copy.start()
    for copy in copies:
        copy.wait()


def shards(
    tm_n, bat_n, power0, charge0, dyn_dual0, feeder_dual0, price, inflow,
    power_limit, capacity, feeder_limit, block_values, block_cols, block_offsets,
):
    rows, cols = power0.shape
    stored, blk, _ = block_values.shape
    feed_rows, feed_cols = feeder_dual0.shape
    own, feed_blocks = cols // blk, feed_cols // blk
    group = own * (rows // 8) + 1
    vmem = pl.BlockSpec(memory_space=pltpu.VMEM)
    dma = pltpu.SemaphoreType.DMA
    state = jax.ShapeDtypeStruct((rows, cols), F32)
    outs = (state, state, state, jax.ShapeDtypeStruct((feed_rows, feed_cols), F32))
    hbm = pl.BlockSpec(memory_space=pltpu.HBM)
    operands = (
        power0, charge0, dyn_dual0, feeder_dual0, price, inflow,
        power_limit, capacity, feeder_limit, block_values, block_cols, block_offsets,
    )
    results = pl.pallas_call(
        functools.partial(kernel, tm_n, bat_n),
        out_shape=outs,
        in_specs=[hbm] * len(operands),
        out_specs=(vmem,) * 4,
        scratch_shapes=[
            *[pltpu.VMEM(x.shape, x.dtype) for x in operands[:10]],
            *[pltpu.SMEM(x.shape, x.dtype) for x in operands[10:]],
            dma((len(operands),)),
            pltpu.VMEM((bat_n, feed_rows, feed_cols), F32),
            pltpu.VMEM((ITERS, bat_n * group, 8, blk), F32),
            pltpu.VMEM((bat_n * own, 2 * rows, blk), BF16),
            pltpu.VMEM((feed_blocks, 2 * rows, blk), BF16),
            pltpu.VMEM((stored + 1, rows, blk), F32),
            pltpu.VMEM((stored, 2 * blk, blk), BF16),
            pltpu.VMEM((stored, blk, 2 * blk), BF16),
            pltpu.VMEM((ITERS - 1, tm_n, 2, blk), F32),
            pltpu.VMEM((ITERS, 1, cols), F32),
            pltpu.VMEM((ITERS, 1, cols), F32),
            pltpu.VMEM((1, cols), F32),
            pltpu.VMEM((ITERS, 1, cols), F32),
            pltpu.VMEM((ITERS, 1, cols), F32),
            pltpu.VMEM((1, cols), F32),
            pltpu.VMEM((bat_n, feed_rows, feed_cols), F32),
            dma((bat_n - 1,)), dma((bat_n - 1,)),
            dma((ITERS, bat_n - 1)), dma((ITERS, bat_n - 1)),
            dma((ITERS - 1, tm_n - 1)), dma((ITERS - 1, tm_n - 1)),
            dma((2 * ITERS + 1,)), dma((2 * ITERS + 1,)),
        ],
        compiler_params=pltpu.CompilerParams(
            collective_id=0, has_side_effects=True, vmem_limit_bytes=VMEM_BYTES
        ),
    )(*operands)
    return pl.pallas_call(
        hand_over,
        out_shape=outs,
        in_specs=[hbm] * 4,
        out_specs=(hbm,) * 4,
        scratch_shapes=[dma((4,))],
        compiler_params=pltpu.CompilerParams(vmem_limit_bytes=VMEM_BYTES),
    )(*results)


def solution(mesh):
    state = P("tm", "bat")
    duals = P(("tm", "bat"), None)
    return jax.shard_map(
        functools.partial(shards, mesh.shape["tm"], mesh.shape["bat"]),
        mesh=mesh,
        in_specs=(state, state, state, duals, state, state, P("bat"), P("bat"), P(), P(), P(), P()),
        out_specs=(state, state, state, duals),
        check_vma=False,
    )
```

```python
import functools

import jax
import jax.numpy as jnp
from jax import lax
from jax.experimental import pallas as pl
from jax.experimental.pallas import tpu as pltpu
from jax.sharding import PartitionSpec as P

ITERS = 4
ETA_STEP = 0.4
EPS_NORM = 1e-06
VMEM_BYTES = 64 * 1024 * 1024
MESH = pl.DeviceIdType.MESH
F32, BF16 = jnp.float32, jnp.bfloat16


def split(x):
    high = x.astype(BF16)
    return high, (x - high.astype(F32)).astype(BF16)


def stacked(x, axis):
    return jnp.concatenate(split(x), axis=axis)


def quadrants(out, rows, blk):
    return out[:rows, :blk] + (out[rows:, :blk] + out[:rows, blk:])


def kernel(
    tm_n, bat_n,
    power_in, charge_in, dyn_in, feed_in, price_in, inflow_in,
    limit_in, capacity_in, feed_limit_in, values_in, cols_in, offsets_in,
    power_out, charge_out, dyn_out, feed_out,
    power_ref, charge_ref, dyn_ref, feed_ref, price_ref, inflow_ref,
    limit_ref, capacity_ref, feed_limit_ref, values_ref, cols_ref, offsets_ref, fetch_sem,
    feed_all, early, bars, late, bar_parts, feed_parts, running, by_rows, by_cols,
    sums, row_next, row_prev, row_charge, own_first, own_last, own_charge, feed_own, results,
    feed_send, feed_recv, early_send, early_recv, bar_send, bar_recv, late_send, late_recv,
    sum_send, sum_recv, edge_send, edge_recv, cross_send, cross_recv,
):
    me_t, me_b = lax.axis_index("tm"), lax.axis_index("bat")
    pairs = (
        (feed_in, feed_ref), (dyn_in, dyn_ref), (charge_in, charge_ref),
        (power_in, power_ref), (price_in, price_ref), (inflow_in, inflow_ref),
        (limit_in, limit_ref), (capacity_in, capacity_ref),
        (cols_in, cols_ref), (offsets_in, offsets_ref), (feed_limit_in, feed_limit_ref),
        (values_in, values_ref),
    )
    fetches = [pltpu.make_async_copy(a, b, fetch_sem.at[i]) for i, (a, b) in enumerate(pairs)]
    for copy in fetches:
        copy.start()
    rows, cols = power_ref.shape
    stored, blk, _ = values_ref.shape
    own = cols // blk
    blocks = bat_n * own
    feed_blocks = feed_ref.shape[1] // blk
    feed_rows = feed_ref.shape[0]
    base = me_b * own

    def at(t, b):
        return (lax.rem(me_t + t, tm_n), lax.rem(me_b + b, bat_n))

    before_t, after_t = tm_n - 1, 1
    partners = (
        [(0, d) for d in range(1, bat_n)]
        + [(d, 0) for d in range(1, tm_n)]
        + [(t, d) for t in (before_t, after_t) for d in range(1, bat_n)]
    )
    barrier = pltpu.get_barrier_semaphore()
    for t, b in partners:
        pl.semaphore_signal(barrier, inc=1, device_id=at(t, b), device_id_type=MESH)
    pl.semaphore_wait(barrier, len(partners))

    started = []

    def send(src, dst, send_sem, recv_sem, device):
        copy = pltpu.make_async_remote_copy(
            src_ref=src, dst_ref=dst, send_sem=send_sem, recv_sem=recv_sem,
            device_id=device, device_id_type=MESH,
        )
        copy.start()
        started.append(copy)
        return copy

    def spread(ref, send_sems, recv_sems):
        mine = ref.at[pl.ds(base, own)]
        return [
            send(mine, mine, send_sems.at[d - 1], recv_sems.at[d - 1], at(0, d))
            for d in range(1, bat_n)
        ]

    def in_blocks(ref):
        return jnp.stack([ref[:, k * blk:(k + 1) * blk] for k in range(own)], axis=0)

    def row_part(ref, k):
        return ref[k * blk:(k + 1) * blk].reshape(1, blk)

    def row_blocks(ref):
        return jnp.stack([row_part(ref, k) for k in range(own)], axis=0)

    fetches[0].wait()
    feed_copies = [
        send(feed_ref, feed_all.at[me_b], feed_send.at[d - 1], feed_recv.at[d - 1], at(0, d))
        for d in range(1, bat_n)
    ]
    fetches[1].wait()
    fetches[2].wait()
    dyn, charge = in_blocks(dyn_ref), in_blocks(charge_ref)
    mine = pl.ds(base, own)
    own_first[0, mine] = dyn[:, 0:1]
    own_last[0, mine] = dyn[:, rows - 1:rows]
    own_charge[...] = charge[:, rows - 1:rows]

    def send_edges(step, span):
        return [
            send(own_first.at[step, span], row_next.at[step, span],
                 edge_send.at[2 * step], edge_recv.at[2 * step], at(before_t, 0)),
            send(own_last.at[step, span], row_prev.at[step, span],
                 edge_send.at[2 * step + 1], edge_recv.at[2 * step + 1], at(after_t, 0)),
        ]

    edge_copies = send_edges(0, mine) + [
        send(own_charge, row_charge, edge_send.at[2 * ITERS], edge_recv.at[2 * ITERS], at(after_t, 0))
    ]
    for copy in fetches[3:8]:
        copy.wait()
    power, price, inflow = in_blocks(power_ref), in_blocks(price_ref), in_blocks(inflow_ref)
    limit, capacity = row_blocks(limit_ref), row_blocks(capacity_ref)
    early[mine, 0:rows] = price
    early[mine, rows:2 * rows] = inflow
    early[mine, 2 * rows:3 * rows] = power
    early[mine, 3 * rows:3 * rows + 8] = jnp.concatenate(
        [limit, capacity, jnp.zeros((own, 6, blk), F32)], axis=1
    )
    early_copies = spread(early, early_send, early_recv)

    feed_all[me_b] = feed_ref[...]
    for copy in fetches[8:]:
        copy.wait()
    for j in range(stored):
        high, low = split(values_ref[j])
        by_cols[j, :, :blk] = high
        by_cols[j, :, blk:] = low
        by_rows[j, :blk, :] = high
        by_rows[j, blk:, :] = low

    row_of = [
        sum((j >= offsets_ref[f]).astype(jnp.int32) for f in range(1, feed_blocks))
        for j in range(stored)
    ]
    col_of = [cols_ref[j] for j in range(stored)]

    def battery_of(feed, first, count):
        for f in range(feed_blocks):
            feed_parts[f] = stacked(feed[f], 0)
        ids = lax.broadcasted_iota(jnp.int32, (count, rows, blk), 0)
        total = jnp.zeros((count, rows, blk), F32)
        for j in range(stored):
            out = jnp.dot(feed_parts[row_of[j]], by_cols[j], preferred_element_type=F32)
            out = quadrants(out, rows, blk)
            total = total + jnp.where(ids == col_of[j] - first, out[None], 0.0)
        return total

    def feeder_of(bar):
        bar_parts[:, :rows], bar_parts[:, rows:] = split(bar)
        total = jnp.zeros((rows, blk), F32)
        running[0] = total
        for j in range(stored):
            out = lax.dot_general(
                bar_parts[col_of[j]], by_rows[j], (((1,), (1,)), ((), ())),
                preferred_element_type=F32,
            )
            total = total + quadrants(out, rows, blk)
            running[j + 1] = total
        return [running[offsets_ref[f + 1]] - running[offsets_ref[f]] for f in range(feed_blocks)]

    for copy in feed_copies:
        copy.wait_recv()
    feed = [
        jnp.concatenate([feed_all[n, :, f * blk:(f + 1) * blk] for n in range(bat_n)], axis=0)
        for f in range(feed_blocks)
    ]
    pushed = battery_of(feed, base, own)

    for copy in edge_copies:
        copy.wait_recv()

    not_first = jnp.where(me_t == 0, 0.0, 1.0)
    not_last = jnp.where(me_t == tm_n - 1, 0.0, 1.0)
    before = row_charge[...]
    following, preceding = row_next[0, mine], row_prev[0, mine]
    weight = jnp.ones((1, 1, blk), F32)

    for step in range(ITERS):
        last = step + 1 == ITERS
        step_primal = ETA_STEP / weight
        step_dual = ETA_STEP * weight
        index = lax.broadcasted_iota(jnp.int32, power.shape, 1)
        later = jnp.where(index == rows - 1, following * not_last, pltpu.roll(dyn, rows - 1, 1))
        power_new = power - step_primal * (price - dyn + pushed)
        power_new = jnp.minimum(jnp.maximum(power_new, -limit), limit)
        power_bar = 2.0 * power_new - power
        charge_new = charge - step_primal * (dyn - later)
        charge_new = jnp.minimum(jnp.maximum(charge_new, 0.0), capacity)
        before_new = before - step_primal * (preceding - dyn[:, 0:1])
        before_new = jnp.minimum(jnp.maximum(before_new, 0.0), capacity)
        charge_bar = 2.0 * charge_new - charge
        before_bar = (2.0 * before_new - before) * not_first
        earlier = jnp.where(index == 0, before_bar, pltpu.roll(charge_bar, 1, 1))
        dyn_new = dyn + step_dual * (charge_bar - earlier - power_bar - inflow)
        if not last:
            primal = (power_new - power) * (power_new - power) + (charge_new - charge) * (charge_new - charge)
            moved = (dyn_new - dyn) * (dyn_new - dyn)
            first_row, last_row = dyn_new[:, 0:1], dyn_new[:, rows - 1:rows]
        if step == 0:
            bars[mine, 0:rows] = power_bar
            bars[mine, rows:rows + 8] = jnp.concatenate(
                [jnp.sum(primal, axis=1, keepdims=True), jnp.sum(moved, axis=1, keepdims=True),
                 jnp.zeros((own, 6, blk), F32)], axis=1
            )
            bar_copies = spread(bars, bar_send, bar_recv)
            own_first[1, mine] = first_row
            own_last[1, mine] = last_row
            edge_copies = []
            for d in range(bat_n):
                edge_copies += [
                    send(own_first.at[1, mine], row_next.at[1, mine],
                         cross_send.at[0, d], cross_recv.at[0, d], at(before_t, d)),
                    send(own_last.at[1, mine], row_prev.at[1, mine],
                         cross_send.at[1, d], cross_recv.at[1, d], at(after_t, d)),
                ]
            late[mine, 0:rows] = charge_new
            late[mine, rows:2 * rows] = dyn_new
            late[mine, 2 * rows:2 * rows + 8] = jnp.concatenate(
                [before_new, jnp.zeros((own, 7, blk), F32)], axis=1
            )
            late_copies = spread(late, late_send, late_recv)
            for copy in bar_copies:
                copy.wait_recv()
            power_bar = bars[:, 0:rows]
            gathered = jnp.sum(bars[:, rows:rows + 8], axis=0)[0:2]
        elif not last:
            everything = slice(0, blocks)
            own_first[step + 1] = first_row
            own_last[step + 1] = last_row
            edge_copies = send_edges(step + 1, everything)
            gathered = jnp.concatenate(
                [jnp.sum(jnp.sum(primal, axis=0), axis=0, keepdims=True),
                 jnp.sum(jnp.sum(moved, axis=0), axis=0, keepdims=True)], axis=0
            )
        coupled = feeder_of(power_bar)
        flat_dual = step_dual.reshape(1, blk)
        feed_new = [
            jnp.maximum(0.0, feed[f] + flat_dual * (coupled[f] - row_part(feed_limit_ref, f)))
            for f in range(feed_blocks)
        ]
        if not last:
            change = jnp.zeros((rows, blk), F32)
            for f in range(feed_blocks):
                change = change + (feed_new[f] - feed[f]) * (feed_new[f] - feed[f])
            change = jnp.sum(change, axis=0, keepdims=True)
            sums[step, me_t] = jnp.concatenate([gathered[0:1], gathered[1:2] + change], axis=0)
            total = sums.at[step, me_t]
            sum_copies = [
                send(total, total, sum_send.at[step, d - 1], sum_recv.at[step, d - 1], at(d, 0))
                for d in range(1, tm_n)
            ]
            pushed = battery_of(feed_new, 0, blocks)
            if step == 0:
                for copy in early_copies + late_copies:
                    copy.wait_recv()
                price, inflow = early[:, 0:rows], early[:, rows:2 * rows]
                power_new = 0.5 * (power_bar + early[:, 2 * rows:3 * rows])
                limit = early[:, 3 * rows:3 * rows + 1]
                capacity = early[:, 3 * rows + 1:3 * rows + 2]
                charge_new, dyn_new = late[:, 0:rows], late[:, rows:2 * rows]
                before_new = late[:, 2 * rows:2 * rows + 1]
            for copy in edge_copies + sum_copies:
                copy.wait_recv()
            following, preceding = row_next[step + 1], row_prev[step + 1]
            both = sums[step, 0]
            for t in range(1, tm_n):
                both = both + sums[step, t]
            both = jnp.sum(both, axis=1, keepdims=True) + EPS_NORM
            ratio = jnp.sqrt(jnp.broadcast_to(both[1:2], (1, blk)) / jnp.broadcast_to(both[0:1], (1, blk)))
            weight = jnp.sqrt(weight * ratio.reshape(1, 1, blk))
        power, charge, dyn, before, feed = power_new, charge_new, dyn_new, before_new, feed_new
        if step == ITERS - 1:
            for n, value in enumerate((power, charge, dyn)):
                results[n] = value

    for n, out in enumerate((power_out, charge_out, dyn_out)):
        for k in range(own):
            out[:, k * blk:(k + 1) * blk] = results[n, base + k]
    for n in range(bat_n):
        for f in range(feed_blocks):
            feed_own[n, :, f * blk:(f + 1) * blk] = feed[f][n * feed_rows:(n + 1) * feed_rows]
    feed_out[...] = feed_own[me_b]
    for copy in started:
        copy.wait_send()


def hand_over(*refs):
    half = len(refs) // 2
    for source, out in zip(refs[:half], refs[half:]):
        out[...] = source[...]


def shards(
    tm_n, bat_n, power0, charge0, dyn_dual0, feeder_dual0, price, inflow,
    power_limit, capacity, feeder_limit, block_values, block_cols, block_offsets,
):
    rows, cols = power0.shape
    stored, blk, _ = block_values.shape
    feed_rows, feed_cols = feeder_dual0.shape
    own, feed_blocks = cols // blk, feed_cols // blk
    blocks = bat_n * own
    vmem = pl.BlockSpec(memory_space=pltpu.VMEM)
    dma = pltpu.SemaphoreType.DMA
    state = jax.ShapeDtypeStruct((rows, cols), F32)
    outs = (state, state, state, jax.ShapeDtypeStruct((feed_rows, feed_cols), F32))
    hbm = pl.BlockSpec(memory_space=pltpu.HBM)
    operands = (
        power0, charge0, dyn_dual0, feeder_dual0, price, inflow,
        power_limit, capacity, feeder_limit, block_values, block_cols, block_offsets,
    )
    results = pl.pallas_call(
        functools.partial(kernel, tm_n, bat_n),
        out_shape=outs,
        in_specs=[hbm] * len(operands),
        out_specs=(vmem,) * 4,
        scratch_shapes=[
            *[pltpu.VMEM(x.shape, x.dtype) for x in operands[:10]],
            *[pltpu.SMEM(x.shape, x.dtype) for x in operands[10:]],
            dma((len(operands),)),
            pltpu.VMEM((bat_n, feed_rows, feed_cols), F32),
            pltpu.VMEM((blocks, 3 * rows + 8, blk), F32),
            pltpu.VMEM((blocks, rows + 8, blk), F32),
            pltpu.VMEM((blocks, 2 * rows + 8, blk), F32),
            pltpu.VMEM((blocks, 2 * rows, blk), BF16),
            pltpu.VMEM((feed_blocks, 2 * rows, blk), BF16),
            pltpu.VMEM((stored + 1, rows, blk), F32),
            pltpu.VMEM((stored, 2 * blk, blk), BF16),
            pltpu.VMEM((stored, blk, 2 * blk), BF16),
            pltpu.VMEM((ITERS - 1, tm_n, 2, blk), F32),
            pltpu.VMEM((ITERS, blocks, 1, blk), F32),
            pltpu.VMEM((ITERS, blocks, 1, blk), F32),
            pltpu.VMEM((own, 1, blk), F32),
            pltpu.VMEM((ITERS, blocks, 1, blk), F32),
            pltpu.VMEM((ITERS, blocks, 1, blk), F32),
            pltpu.VMEM((own, 1, blk), F32),
            pltpu.VMEM((bat_n, feed_rows, feed_cols), F32),
            pltpu.VMEM((3, blocks, rows, blk), F32),
            *[dma((bat_n - 1,)) for _ in range(8)],
            dma((ITERS - 1, tm_n - 1)), dma((ITERS - 1, tm_n - 1)),
            dma((2 * ITERS + 1,)), dma((2 * ITERS + 1,)),
            dma((2, bat_n)), dma((2, bat_n)),
        ],
        compiler_params=pltpu.CompilerParams(
            collective_id=0, has_side_effects=True, vmem_limit_bytes=VMEM_BYTES
        ),
    )(*operands)
    return pl.pallas_call(
        hand_over,
        out_shape=outs,
        in_specs=[vmem] * 4,
        out_specs=(vmem,) * 4,
        compiler_params=pltpu.CompilerParams(vmem_limit_bytes=VMEM_BYTES),
    )(*results)


def solution(mesh):
    state = P("tm", "bat")
    duals = P(("tm", "bat"), None)
    return jax.shard_map(
        functools.partial(shards, mesh.shape["tm"], mesh.shape["bat"]),
        mesh=mesh,
        in_specs=(state, state, state, duals, state, state, P("bat"), P("bat"), P(), P(), P(), P()),
        out_specs=(state, state, state, duals),
        check_vma=False,
    )
```

```python
import functools

import jax
import jax.numpy as jnp
from jax import lax
from jax.experimental import pallas as pl
from jax.experimental.pallas import tpu as pltpu
from jax.sharding import PartitionSpec as P

ITERS = 4
ETA_STEP = 0.4
EPS_NORM = 1e-06
VMEM_BYTES = 64 * 1024 * 1024
MESH = pl.DeviceIdType.MESH
F32, BF16 = jnp.float32, jnp.bfloat16


def split(x):
    high = x.astype(BF16)
    return high, (x - high.astype(F32)).astype(BF16)


def stacked(x, axis):
    return jnp.concatenate(split(x), axis=axis)


def quadrants(out, rows, blk):
    return out[:rows, :blk] + (out[rows:, :blk] + out[:rows, blk:])


def kernel(
    tm_n, bat_n,
    power_in, charge_in, dyn_in, feed_in, price_in, inflow_in,
    limit_in, capacity_in, feed_limit_in, values_in, cols_in, offsets_in,
    power_out, charge_out, dyn_out, feed_out,
    power_ref, charge_ref, dyn_ref, feed_ref, price_ref, inflow_ref,
    limit_ref, capacity_ref, feed_limit_ref, values_ref, cols_ref, offsets_ref, fetch_sem,
    feed_all, early, bars, late, bar_parts, feed_parts, running, by_rows, by_cols,
    sums, row_next, row_prev, row_charge, own_first, own_last, own_charge, feed_own, results,
    feed_send, feed_recv, early_send, early_recv, bar_send, bar_recv, late_send, late_recv,
    sum_send, sum_recv, edge_send, edge_recv, cross_send, cross_recv,
):
    me_t, me_b = lax.axis_index("tm"), lax.axis_index("bat")
    pairs = (
        (feed_in, feed_ref), (dyn_in, dyn_ref), (charge_in, charge_ref),
        (power_in, power_ref), (price_in, price_ref), (inflow_in, inflow_ref),
        (limit_in, limit_ref), (capacity_in, capacity_ref),
        (cols_in, cols_ref), (offsets_in, offsets_ref), (feed_limit_in, feed_limit_ref),
        (values_in, values_ref),
    )
    fetches = [pltpu.make_async_copy(a, b, fetch_sem.at[i]) for i, (a, b) in enumerate(pairs)]
    for copy in fetches:
        copy.start()
    rows, cols = power_ref.shape
    stored, blk, _ = values_ref.shape
    own = cols // blk
    blocks = bat_n * own
    feed_blocks = feed_ref.shape[1] // blk
    feed_rows = feed_ref.shape[0]
    base = me_b * own

    def at(t, b):
        return (lax.rem(me_t + t, tm_n), lax.rem(me_b + b, bat_n))

    before_t, after_t = tm_n - 1, 1
    partners = (
        [(0, d) for d in range(1, bat_n)]
        + [(d, 0) for d in range(1, tm_n)]
        + [(t, d) for t in (before_t, after_t) for d in range(1, bat_n)]
    )
    barrier = pltpu.get_barrier_semaphore()
    for t, b in partners:
        pl.semaphore_signal(barrier, inc=1, device_id=at(t, b), device_id_type=MESH)

    started = []

    def send(src, dst, send_sem, recv_sem, device):
        copy = pltpu.make_async_remote_copy(
            src_ref=src, dst_ref=dst, send_sem=send_sem, recv_sem=recv_sem,
            device_id=device, device_id_type=MESH,
        )
        copy.start()
        started.append(copy)
        return copy

    def spread(ref, send_sems, recv_sems):
        mine = ref.at[pl.ds(base, own)]
        return [
            send(mine, mine, send_sems.at[d - 1], recv_sems.at[d - 1], at(0, d))
            for d in range(1, bat_n)
        ]

    def in_blocks(ref):
        return jnp.stack([ref[:, k * blk:(k + 1) * blk] for k in range(own)], axis=0)

    def row_part(ref, k):
        return ref[k * blk:(k + 1) * blk].reshape(1, blk)

    def row_blocks(ref):
        return jnp.stack([row_part(ref, k) for k in range(own)], axis=0)

    fetches[0].wait()
    fetches[1].wait()
    fetches[2].wait()
    dyn, charge = in_blocks(dyn_ref), in_blocks(charge_ref)
    mine = pl.ds(base, own)
    own_first[0, mine] = dyn[:, 0:1]
    own_last[0, mine] = dyn[:, rows - 1:rows]
    own_charge[...] = charge[:, rows - 1:rows]

    def send_edges(step, span):
        return [
            send(own_first.at[step, span], row_next.at[step, span],
                 edge_send.at[2 * step], edge_recv.at[2 * step], at(before_t, 0)),
            send(own_last.at[step, span], row_prev.at[step, span],
                 edge_send.at[2 * step + 1], edge_recv.at[2 * step + 1], at(after_t, 0)),
        ]

    for copy in fetches[3:8]:
        copy.wait()
    power, price, inflow = in_blocks(power_ref), in_blocks(price_ref), in_blocks(inflow_ref)
    limit, capacity = row_blocks(limit_ref), row_blocks(capacity_ref)
    early[mine, 0:rows] = price
    early[mine, rows:2 * rows] = inflow
    early[mine, 2 * rows:3 * rows] = power
    early[mine, 3 * rows:3 * rows + 8] = jnp.concatenate(
        [limit, capacity, jnp.zeros((own, 6, blk), F32)], axis=1
    )
    pl.semaphore_wait(barrier, len(partners))
    feed_copies = [
        send(feed_ref, feed_all.at[me_b], feed_send.at[d - 1], feed_recv.at[d - 1], at(0, d))
        for d in range(1, bat_n)
    ]
    edge_copies = send_edges(0, mine) + [
        send(own_charge, row_charge, edge_send.at[2 * ITERS], edge_recv.at[2 * ITERS], at(after_t, 0))
    ]
    early_copies = spread(early, early_send, early_recv)

    feed_all[me_b] = feed_ref[...]
    for copy in fetches[8:]:
        copy.wait()
    for j in range(stored):
        high, low = split(values_ref[j])
        by_cols[j, :, :blk] = high
        by_cols[j, :, blk:] = low
        by_rows[j, :blk, :] = high
        by_rows[j, blk:, :] = low

    row_of = [
        sum((j >= offsets_ref[f]).astype(jnp.int32) for f in range(1, feed_blocks))
        for j in range(stored)
    ]
    col_of = [cols_ref[j] for j in range(stored)]

    def battery_of(feed, first, count):
        for f in range(feed_blocks):
            feed_parts[f] = stacked(feed[f], 0)
        ids = lax.broadcasted_iota(jnp.int32, (count, rows, blk), 0)
        total = jnp.zeros((count, rows, blk), F32)
        for j in range(stored):
            out = jnp.dot(feed_parts[row_of[j]], by_cols[j], preferred_element_type=F32)
            out = quadrants(out, rows, blk)
            total = total + jnp.where(ids == col_of[j] - first, out[None], 0.0)
        return total

    def feeder_of(bar):
        bar_parts[:, :rows], bar_parts[:, rows:] = split(bar)
        total = jnp.zeros((rows, blk), F32)
        running[0] = total
        for j in range(stored):
            out = lax.dot_general(
                bar_parts[col_of[j]], by_rows[j], (((1,), (1,)), ((), ())),
                preferred_element_type=F32,
            )
            total = total + quadrants(out, rows, blk)
            running[j + 1] = total
        return [running[offsets_ref[f + 1]] - running[offsets_ref[f]] for f in range(feed_blocks)]

    for copy in feed_copies:
        copy.wait_recv()
    feed = [
        jnp.concatenate([feed_all[n, :, f * blk:(f + 1) * blk] for n in range(bat_n)], axis=0)
        for f in range(feed_blocks)
    ]
    pushed = battery_of(feed, base, own)

    for copy in edge_copies:
        copy.wait_recv()

    not_first = jnp.where(me_t == 0, 0.0, 1.0)
    not_last = jnp.where(me_t == tm_n - 1, 0.0, 1.0)
    before = row_charge[...]
    following, preceding = row_next[0, mine], row_prev[0, mine]
    weight = jnp.ones((1, 1, blk), F32)

    for step in range(ITERS):
        last = step + 1 == ITERS
        step_primal = ETA_STEP / weight
        step_dual = ETA_STEP * weight
        index = lax.broadcasted_iota(jnp.int32, power.shape, 1)
        later = jnp.where(index == rows - 1, following * not_last, pltpu.roll(dyn, rows - 1, 1))
        power_new = power - step_primal * (price - dyn + pushed)
        power_new = jnp.minimum(jnp.maximum(power_new, -limit), limit)
        power_bar = 2.0 * power_new - power
        charge_new = charge - step_primal * (dyn - later)
        charge_new = jnp.minimum(jnp.maximum(charge_new, 0.0), capacity)
        before_new = before - step_primal * (preceding - dyn[:, 0:1])
        before_new = jnp.minimum(jnp.maximum(before_new, 0.0), capacity)
        charge_bar = 2.0 * charge_new - charge
        before_bar = (2.0 * before_new - before) * not_first
        earlier = jnp.where(index == 0, before_bar, pltpu.roll(charge_bar, 1, 1))
        dyn_new = dyn + step_dual * (charge_bar - earlier - power_bar - inflow)
        if not last:
            primal = (power_new - power) * (power_new - power) + (charge_new - charge) * (charge_new - charge)
            moved = (dyn_new - dyn) * (dyn_new - dyn)
            first_row, last_row = dyn_new[:, 0:1], dyn_new[:, rows - 1:rows]
        if step == 0:
            bars[mine, 0:rows] = power_bar
            bars[mine, rows:rows + 8] = jnp.concatenate(
                [jnp.sum(primal, axis=1, keepdims=True), jnp.sum(moved, axis=1, keepdims=True),
                 jnp.zeros((own, 6, blk), F32)], axis=1
            )
            bar_copies = spread(bars, bar_send, bar_recv)
            own_first[1, mine] = first_row
            own_last[1, mine] = last_row
            edge_copies = []
            for d in range(bat_n):
                edge_copies += [
                    send(own_first.at[1, mine], row_next.at[1, mine],
                         cross_send.at[0, d], cross_recv.at[0, d], at(before_t, d)),
                    send(own_last.at[1, mine], row_prev.at[1, mine],
                         cross_send.at[1, d], cross_recv.at[1, d], at(after_t, d)),
                ]
            late[mine, 0:rows] = charge_new
            late[mine, rows:2 * rows] = dyn_new
            late[mine, 2 * rows:2 * rows + 8] = jnp.concatenate(
                [before_new, jnp.zeros((own, 7, blk), F32)], axis=1
            )
            late_copies = spread(late, late_send, late_recv)
            for copy in bar_copies:
                copy.wait_recv()
            power_bar = bars[:, 0:rows]
            gathered = jnp.sum(bars[:, rows:rows + 8], axis=0)[0:2]
        elif not last:
            everything = slice(0, blocks)
            own_first[step + 1] = first_row
            own_last[step + 1] = last_row
            edge_copies = send_edges(step + 1, everything)
            gathered = jnp.concatenate(
                [jnp.sum(jnp.sum(primal, axis=0), axis=0, keepdims=True),
                 jnp.sum(jnp.sum(moved, axis=0), axis=0, keepdims=True)], axis=0
            )
        coupled = feeder_of(power_bar)
        flat_dual = step_dual.reshape(1, blk)
        feed_new = [
            jnp.maximum(0.0, feed[f] + flat_dual * (coupled[f] - row_part(feed_limit_ref, f)))
            for f in range(feed_blocks)
        ]
        if not last:
            change = jnp.zeros((rows, blk), F32)
            for f in range(feed_blocks):
                change = change + (feed_new[f] - feed[f]) * (feed_new[f] - feed[f])
            change = jnp.sum(change, axis=0, keepdims=True)
            sums[step, me_t] = jnp.concatenate([gathered[0:1], gathered[1:2] + change], axis=0)
            total = sums.at[step, me_t]
            sum_copies = [
                send(total, total, sum_send.at[step, d - 1], sum_recv.at[step, d - 1], at(d, 0))
                for d in range(1, tm_n)
            ]
            pushed = battery_of(feed_new, 0, blocks)
            if step == 0:
                for copy in early_copies + late_copies:
                    copy.wait_recv()
                price, inflow = early[:, 0:rows], early[:, rows:2 * rows]
                power_new = 0.5 * (power_bar + early[:, 2 * rows:3 * rows])
                limit = early[:, 3 * rows:3 * rows + 1]
                capacity = early[:, 3 * rows + 1:3 * rows + 2]
                charge_new, dyn_new = late[:, 0:rows], late[:, rows:2 * rows]
                before_new = late[:, 2 * rows:2 * rows + 1]
            for copy in edge_copies + sum_copies:
                copy.wait_recv()
            following, preceding = row_next[step + 1], row_prev[step + 1]
            both = sums[step, 0]
            for t in range(1, tm_n):
                both = both + sums[step, t]
            both = jnp.sum(both, axis=1, keepdims=True) + EPS_NORM
            ratio = jnp.sqrt(jnp.broadcast_to(both[1:2], (1, blk)) / jnp.broadcast_to(both[0:1], (1, blk)))
            weight = jnp.sqrt(weight * ratio.reshape(1, 1, blk))
        power, charge, dyn, before, feed = power_new, charge_new, dyn_new, before_new, feed_new
        if step == ITERS - 1:
            for n, value in enumerate((power, charge, dyn)):
                results[n] = value

    for n, out in enumerate((power_out, charge_out, dyn_out)):
        for k in range(own):
            out[:, k * blk:(k + 1) * blk] = results[n, base + k]
    for n in range(bat_n):
        for f in range(feed_blocks):
            feed_own[n, :, f * blk:(f + 1) * blk] = feed[f][n * feed_rows:(n + 1) * feed_rows]
    feed_out[...] = feed_own[me_b]
    for copy in started:
        copy.wait_send()


def hand_over(*refs):
    half = len(refs) // 2
    for source, out in zip(refs[:half], refs[half:]):
        out[...] = source[...]


def shards(
    tm_n, bat_n, power0, charge0, dyn_dual0, feeder_dual0, price, inflow,
    power_limit, capacity, feeder_limit, block_values, block_cols, block_offsets,
):
    rows, cols = power0.shape
    stored, blk, _ = block_values.shape
    feed_rows, feed_cols = feeder_dual0.shape
    own, feed_blocks = cols // blk, feed_cols // blk
    blocks = bat_n * own
    vmem = pl.BlockSpec(memory_space=pltpu.VMEM)
    dma = pltpu.SemaphoreType.DMA
    state = jax.ShapeDtypeStruct((rows, cols), F32)
    outs = (state, state, state, jax.ShapeDtypeStruct((feed_rows, feed_cols), F32))
    hbm = pl.BlockSpec(memory_space=pltpu.HBM)
    operands = (
        power0, charge0, dyn_dual0, feeder_dual0, price, inflow,
        power_limit, capacity, feeder_limit, block_values, block_cols, block_offsets,
    )
    results = pl.pallas_call(
        functools.partial(kernel, tm_n, bat_n),
        out_shape=outs,
        in_specs=[hbm] * len(operands),
        out_specs=(vmem,) * 4,
        scratch_shapes=[
            *[pltpu.VMEM(x.shape, x.dtype) for x in operands[:10]],
            *[pltpu.SMEM(x.shape, x.dtype) for x in operands[10:]],
            dma((len(operands),)),
            pltpu.VMEM((bat_n, feed_rows, feed_cols), F32),
            pltpu.VMEM((blocks, 3 * rows + 8, blk), F32),
            pltpu.VMEM((blocks, rows + 8, blk), F32),
            pltpu.VMEM((blocks, 2 * rows + 8, blk), F32),
            pltpu.VMEM((blocks, 2 * rows, blk), BF16),
            pltpu.VMEM((feed_blocks, 2 * rows, blk), BF16),
            pltpu.VMEM((stored + 1, rows, blk), F32),
            pltpu.VMEM((stored, 2 * blk, blk), BF16),
            pltpu.VMEM((stored, blk, 2 * blk), BF16),
            pltpu.VMEM((ITERS - 1, tm_n, 2, blk), F32),
            pltpu.VMEM((ITERS, blocks, 1, blk), F32),
            pltpu.VMEM((ITERS, blocks, 1, blk), F32),
            pltpu.VMEM((own, 1, blk), F32),
            pltpu.VMEM((ITERS, blocks, 1, blk), F32),
            pltpu.VMEM((ITERS, blocks, 1, blk), F32),
            pltpu.VMEM((own, 1, blk), F32),
            pltpu.VMEM((bat_n, feed_rows, feed_cols), F32),
            pltpu.VMEM((3, blocks, rows, blk), F32),
            *[dma((bat_n - 1,)) for _ in range(8)],
            dma((ITERS - 1, tm_n - 1)), dma((ITERS - 1, tm_n - 1)),
            dma((2 * ITERS + 1,)), dma((2 * ITERS + 1,)),
            dma((2, bat_n)), dma((2, bat_n)),
        ],
        compiler_params=pltpu.CompilerParams(
            collective_id=0, has_side_effects=True, vmem_limit_bytes=VMEM_BYTES
        ),
    )(*operands)
    return pl.pallas_call(
        hand_over,
        out_shape=outs,
        in_specs=[vmem] * 4,
        out_specs=(vmem,) * 4,
        compiler_params=pltpu.CompilerParams(vmem_limit_bytes=VMEM_BYTES),
    )(*results)


def solution(mesh):
    state = P("tm", "bat")
    duals = P(("tm", "bat"), None)
    return jax.shard_map(
        functools.partial(shards, mesh.shape["tm"], mesh.shape["bat"]),
        mesh=mesh,
        in_specs=(state, state, state, duals, state, state, P("bat"), P("bat"), P(), P(), P(), P()),
        out_specs=(state, state, state, duals),
        check_vma=False,
    )
```
